32 devices in a mesh: ctx: 8 (over y, x, core), tp: 4 (over z).
Axes of the slice: x: 2, y: 2, z: 4, core: 2. Of those that a mesh axis runs over, the one named last changes fastest.
Arguments:
- queries: bfloat16 [2048, 4096], P('ctx', 'tp'), may hold values from -12 to 12, as said below
- key_rows: bfloat16 [2048, 1024], P('ctx', 'tp'), may hold values from -12 to 12, as said below
- value_rows: bfloat16 [2048, 1024], P('ctx', 'tp'), may hold values from -6 to 6
- segments: int32 [2048], replicated, may hold values from 0 to 15, never falling along the last dimension, each value on 1 to 1024 neighbouring positions
- owner_ids: int32 [2048, 1], P('ctx'), may hold values from 0 to 3; in each aligned block of 256 rows (0 to 255, 256 to 511, ...) at most 64 rows name the same one
- out_proj: bfloat16 [4096, 8192], P('tp'), may hold values from -0.09375 to 0.09375
- residual: bfloat16 [2048, 8192], P(('ctx', 'tp')), may hold values from -4 to 4
- norm_gain: float32 [8192], replicated, may hold values from 0.5 to 1.5
Outputs:
- hidden_out: bfloat16 [2048, 8192], P(('ctx', 'tp'))
- normed: bfloat16 [2048, 8192], P(('ctx', 'tp'))
The draws below stay inside these ranges and needn't reach their ends.
Inputs may be any that keep to these rules, and one draw needn't show every extreme that they name: `segments`: never falling along the tokens; every document has 1 to 1024 tokens and one has exactly 1024. `owner_ids`: among the rows of one device's token block no owner is named more than 64 times; some owner is named exactly 64 times in some block. `queries`: Real-valued entries. `key_rows`: Real-valued entries.
All inputs are finite; a program needn't handle non-finite values.
Results may differ from the reference program's by a relative error of at most 0.01.
Values may be sent and summed in bfloat16 or wider, within the bound.
A program may use at most 128 MiB of HBM per device.

```python
import math
import jax
import jax.numpy as jnp
import numpy as np
from jax import lax

D = 8192
HEADS = 32
KV_HEADS = 8
HEAD_DIM = 128
TOK_DEV = 256
CAP = 64
TOKENS = 2048
SLOTS = 2048
DOCS = 16
DOC_MOST = 1024
N_CTX = 8
N_TP = 4


def shared_draw(key):
    base_key = jax.random.fold_in(key, 11)
    first_key, second_key = jax.random.split(base_key, 2)
    query_draw = jax.random.normal(first_key, (TOKENS, HEADS * HEAD_DIM), jnp.float32)
    key_draw = jax.random.normal(second_key, (TOKENS, KV_HEADS * HEAD_DIM), jnp.float32)
    return (query_draw, key_draw)


def draw_queries(key, part):
    return shared_draw(key)[0].astype(jnp.bfloat16)


def draw_key_rows(key, part):
    return shared_draw(key)[1].astype(jnp.bfloat16)


def block_scale(own_key, extent, pieces, low, high):
    level, own = 1.0, jax.random.fold_in(own_key, 6)
    for position, parts in pieces:
        steps = jnp.exp(jax.random.uniform(jax.random.fold_in(own, position), (parts,), jnp.float32, low / len(pieces), high / len(pieces)))
        level = level * jnp.repeat(steps, extent[position] // parts).reshape([-1 if axis == position else 1 for axis in range(len(extent))])
    return level


def length_profile(count, total, reach, slope):
    portions = [(1 << 20) // math.isqrt(standing ** slope) + 1 for standing in range(2, count + 1)]
    surplus, given = total - reach - (count - 1), [1] * (count - 1)
    while surplus > 0:
        movable = [i for i in range(count - 1) if given[i] < reach]
        mass, remaining = sum([portions[i] for i in movable]), surplus
        for i in movable:
            addition = min(reach - given[i], max(1, remaining * portions[i] // mass), surplus)
            given[i] = given[i] + addition
            surplus = surplus - addition
    return np.array([reach] + given)


def ragged_sizes(rng, count, total, most, lean):
    if count == 2:
        one = jax.random.randint(rng, (), max(1, total - most), min(most, total - 1) + 1)
        return jnp.stack([one, total - one])
    tallies = jnp.asarray(length_profile(count, total, most, lean), jnp.int32)
    twos = (count - 1) // 2
    donor, receiver = tallies[1:1 + 2 * twos:2], tallies[2:2 + 2 * twos:2]
    margin = jnp.minimum(donor - 1, most - receiver)
    moved = jax.random.randint(jax.random.fold_in(rng, 1), (twos,), 0, 1 << 20) % (margin + 1)
    tallies = tallies.at[1:1 + 2 * twos:2].set(donor - moved).at[2:2 + 2 * twos:2].set(receiver + moved)
    return tallies[jax.random.permutation(jax.random.fold_in(rng, 2), count)]


def assign_block(stream_key, own, number, rows, amount, top, most, lean):
    ranking = jax.random.permutation(stream_key, amount)
    packed, usual = portions_of(amount, rows * top, most, lean, True), portions_of(amount, rows * top, most, lean, False)
    places = jnp.arange(amount)

    def named(lengths, rotation):
        used = int((lengths > 0).sum())
        fixed = max(1, used // 4)
        passed = fixed + (places - fixed + rotation * (used - fixed)) % max(1, amount - fixed)
        return jnp.zeros((amount,), jnp.int32).at[ranking[jnp.where(places < fixed, places, passed)]].set(jnp.asarray(lengths, jnp.int32))

    lengths = jnp.where(number % 4 == 0, named(packed, number // 4), named(usual, number - number // 4 - 1))
    mixed = jax.random.permutation(jax.random.fold_in(own, 3), amount)
    source_of, taker = mixed[0:amount // 2 * 2:2], mixed[1:amount // 2 * 2:2]
    slack = jnp.minimum(lengths[source_of] - 1, most - lengths[taker]) // 2
    slack = jnp.where((source_of == ranking[0]) | (taker == ranking[0]) | (lengths[taker] == 0), 0, jnp.maximum(slack, 0))
    passed = jax.random.randint(jax.random.fold_in(own, 4), (amount // 2,), 0, 1 << 20) % (slack + 1)
    lengths = lengths.at[source_of].add(-passed).at[taker].add(passed)
    labels = jnp.searchsorted(jnp.cumsum(lengths), jnp.arange(rows * top), side="right").astype(jnp.int32)
    listing = labels.reshape(top, rows).T
    listing = listing[jax.random.permutation(jax.random.fold_in(own, 1), rows)]
    rotation = jax.random.randint(jax.random.fold_in(own, 2), (rows, 1), 0, top)
    return jnp.take_along_axis(listing, (jnp.arange(top)[None, :] + rotation) % top, axis=1)


def portions_of(number_of, total, limit, slope, full):
    loads = [(1 << 20) // math.isqrt(rank ** slope) + 1 for rank in range(1, number_of + 1)]
    largest = limit if full else min(limit, max(-(-total // number_of), total * loads[0] // sum(loads)))
    least = 1 if total - largest >= number_of - 1 else 0
    holding, surplus = [largest] + [least] * (number_of - 1), total - largest - least * (number_of - 1)
    while surplus > 0:
        free = [i for i in range(1, number_of) if holding[i] < largest] or [i for i in range(1, number_of) if holding[i] < limit]
        mass, budget = sum([loads[i] for i in free]), surplus
        for i in free:
            extra = min(limit - holding[i], max(1, budget * loads[i] // mass), surplus)
            holding[i] = holding[i] + extra
            surplus = surplus - extra
    return np.array(holding)


def centred(stream_key, dims, width, most, cuts=(), kind=jnp.bfloat16):
    result = jax.random.normal(stream_key, dims, jnp.float32) * width
    if len(cuts) > 0:
        result = block_scale(stream_key, dims, cuts, -0.22, 0.18) * result
    return jnp.clip(result, min=-most, max=most).astype(kind)


def setup_inputs(seed: int = 0) -> dict:
    arg_keys = jax.random.split(jax.random.key(seed), 9)
    queries = draw_queries(jax.random.fold_in(arg_keys[8], 71), 0)
    key_rows = draw_key_rows(jax.random.fold_in(arg_keys[8], 71), 0)
    value_rows = centred(arg_keys[2], (TOKENS, KV_HEADS * HEAD_DIM), 1.0, 6.0, ((0, 8), (1, 4)))
    segments = jnp.searchsorted(jnp.cumsum(ragged_sizes(arg_keys[3], DOCS, TOKENS, DOC_MOST, 2)), jnp.arange(TOKENS), side="right").astype(jnp.int32)
    owner_ids_keys = jax.random.split(jax.random.fold_in(arg_keys[4], 1), TOKENS // TOK_DEV)
    owner_ids_turns = jax.random.permutation(jax.random.fold_in(arg_keys[4], 3), TOKENS // TOK_DEV)
    owner_ids = jax.vmap(lambda own, number: assign_block(jax.random.fold_in(arg_keys[4], 2), own, number, TOK_DEV, N_TP, 1, CAP, 2))(owner_ids_keys, owner_ids_turns).reshape((TOKENS, 1))
    out_proj = centred(arg_keys[5], (HEADS * HEAD_DIM, D), (HEADS * HEAD_DIM) ** -0.5, 0.09375, ((0, 4),))
    residual = centred(arg_keys[6], (SLOTS, D), 0.5, 4.0, ((0, 32),))
    norm_gain = jnp.clip(1.0 + 0.1 * jax.random.normal(arg_keys[7], (D,), jnp.float32), 0.5, 1.5)
    return {"queries": queries, "key_rows": key_rows, "value_rows": value_rows, "segments": segments, "owner_ids": owner_ids, "out_proj": out_proj, "residual": residual, "norm_gain": norm_gain}


def reference(queries, key_rows, value_rows, segments, owner_ids, out_proj, residual, norm_gain):
    group_size = HEADS // KV_HEADS
    score_scale = 1.0 / math.sqrt(HEAD_DIM)
    key_all = key_rows.astype(jnp.float32).reshape(TOKENS, KV_HEADS, HEAD_DIM)
    value_all = value_rows.astype(jnp.float32).reshape(TOKENS, KV_HEADS, HEAD_DIM)
    block_rows = min(256, TOKENS)
    positions = jnp.arange(TOKENS, dtype=jnp.int32)

    def attend(block_index):
        first_row = (block_index * block_rows).astype(jnp.int32)
        query_block = lax.dynamic_slice_in_dim(queries, first_row, block_rows, 0).astype(jnp.float32)
        query_block = query_block.reshape(block_rows, KV_HEADS, group_size, HEAD_DIM)
        seg_block = lax.dynamic_slice_in_dim(segments, first_row, block_rows, 0)
        pos_block = first_row + jnp.arange(block_rows, dtype=jnp.int32)
        scores = jnp.einsum('tkgd,skd->kgts', query_block, key_all) * score_scale
        allowed = (seg_block[:, None] == segments[None, :]) & (positions[None, :] <= pos_block[:, None])
        scores = jnp.where(allowed, scores, -1e+30)
        running_max = lax.optimization_barrier(jnp.max(scores, axis=-1, keepdims=True))
        exponent = jnp.where(allowed, jnp.exp(scores - running_max), 0.0)
        totals = lax.optimization_barrier(jnp.sum(exponent, axis=-1))
        weights = exponent.astype(jnp.bfloat16).astype(jnp.float32)
        mixed_heads = jnp.einsum('kgts,skd->kgtd', weights, value_all) / totals[..., None]
        return jnp.transpose(mixed_heads, (2, 0, 1, 3)).reshape(block_rows, HEADS * HEAD_DIM).astype(jnp.bfloat16)
    attended = lax.map(attend, jnp.arange(TOKENS // block_rows, dtype=jnp.int32))
    attended = attended.reshape(TOKENS, HEADS * HEAD_DIM)
    shard_width = HEADS * HEAD_DIM // N_TP
    combined = jnp.zeros((TOKENS, D), jnp.float32)
    for shard_index in range(N_TP):
        lower = shard_index * shard_width
        partial_rows = jnp.dot(attended[:, lower:lower + shard_width], out_proj[lower:lower + shard_width], preferred_element_type=jnp.float32).astype(jnp.bfloat16)
        combined = combined + partial_rows.astype(jnp.float32)
    owners = owner_ids[:, 0]
    onehot = (owners[:, None] == jnp.arange(N_TP, dtype=jnp.int32)[None, :]).astype(jnp.int32)
    onehot = onehot.reshape(N_CTX, TOK_DEV, N_TP)
    before = jnp.cumsum(onehot, axis=1) - onehot
    row_rank = lax.optimization_barrier(jnp.sum(before * onehot, axis=2)).reshape(TOKENS)
    destination = (positions // TOK_DEV * N_TP + owners) * CAP + row_rank
    scattered = jnp.zeros((SLOTS, D), jnp.float32).at[destination].set(combined)
    hidden_sum = residual.astype(jnp.float32) + scattered
    mean_square = lax.optimization_barrier(jnp.mean(hidden_sum * hidden_sum, axis=-1, keepdims=True))
    normed = hidden_sum * lax.rsqrt(mean_square + 1e-05) * norm_gain.astype(jnp.float32)
    return (hidden_sum.astype(jnp.bfloat16), normed.astype(jnp.bfloat16))
```

```python
import functools
import math

import jax
import jax.numpy as jnp
from jax import lax
from jax.experimental import pallas as pl
from jax.experimental.pallas import tpu as pltpu
from jax.sharding import PartitionSpec as P

HEADS = 32
KV_HEADS = 8
HEAD_DIM = 128
GROUP = HEADS // KV_HEADS
TILE = 1024
CHUNK_BLOCKS = 5
MASKED = -1e30


def kernel(
    n_ctx,
    n_tp,
    q_ref,
    k_ref,
    v_ref,
    seg_ref,
    own_col_ref,
    own_row_ref,
    w_ref,
    res_ref,
    gain_ref,
    hid_ref,
    norm_ref,
    kbuf,
    vbuf,
    wbuf,
    attended,
    partial,
    landed,
    hidden,
    kv_send,
    kv_fwd,
    kv_recv,
    w_sem,
    row_send,
    row_recv,
):
    c = lax.axis_index("ctx")
    z = lax.axis_index("tp")
    rows = q_ref.shape[0]
    cap = res_ref.shape[0]
    tiles = wbuf.shape[0]
    window = n_ctx // 2
    kv_local = k_ref.shape[1] // HEAD_DIM
    scale = 1.0 / math.sqrt(HEAD_DIM)
    even = c % 2 == 0
    partner = c + 1 - 2 * (c % 2)
    strides = list(range(2, window + 1, 2))

    def weight_copy(t):
        cols = pl.ds(pl.multiple_of(t * TILE, TILE), TILE)
        return pltpu.make_async_copy(w_ref.at[:, cols], wbuf.at[t], w_sem.at[t])

    for t in range(tiles):
        weight_copy(t).start()

    barrier = pltpu.get_barrier_semaphore()

    def greet(cond, where):
        @pl.when(cond)
        def _():
            pl.semaphore_signal(barrier, inc=1, device_id=where)

        return cond.astype(jnp.int32)

    expected = 1
    pl.semaphore_signal(barrier, inc=1, device_id={"ctx": partner})
    for r in strides:
        expected = expected + greet(c + r < n_ctx, {"ctx": c + r})
        expected = expected + greet(c >= r, {"ctx": c - r})
    expected = expected + greet(z + 1 < n_tp, {"tp": z + 1})
    expected = expected + greet(z > 0, {"tp": z - 1})
    pl.semaphore_wait(barrier, expected)

    def kv_copies(src, place, send, where):
        dst = pl.ds(place * rows, rows)
        out = []
        for i, (own, buf) in enumerate(((k_ref, kbuf), (v_ref, vbuf))):
            ref = own if src is None else buf.at[pl.ds(src * rows, rows)]
            out.append(
                pltpu.make_async_remote_copy(
                    src_ref=ref,
                    dst_ref=buf.at[dst],
                    send_sem=send.at[i],
                    recv_sem=kv_recv.at[place, i],
                    device_id=where,
                )
            )
        return out

    def own_copies(r):
        return kv_copies(None, window - r, kv_send.at[r], {"ctx": c + r})

    def mate_copies():
        return kv_copies(None, window - 1, kv_send.at[0], {"ctx": partner})

    def forward_copies(r, place):
        return kv_copies(window - r, place, kv_fwd.at[r], {"ctx": partner})

    def landed_copies(r):
        return kv_copies(None, window - r, kv_send.at[r], {"ctx": partner})

    for r in reversed(strides):

        @pl.when(c + r < n_ctx)
        def _():
            for cp in own_copies(r):
                cp.start()

    @pl.when(even)
    def _():
        for cp in mate_copies():
            cp.start()

    kbuf[window * rows :, :] = k_ref[...]
    vbuf[window * rows :, :] = v_ref[...]
    for r in range(1, window + 1):

        @pl.when(c < r)
        def _():
            kbuf[(window - r) * rows : (window - r + 1) * rows, :] = jnp.zeros(k_ref.shape, k_ref.dtype)
            vbuf[(window - r) * rows : (window - r + 1) * rows, :] = jnp.zeros(v_ref.shape, v_ref.dtype)

    earlier = lax.broadcasted_iota(jnp.int32, (rows, rows), 0) < lax.broadcasted_iota(
        jnp.int32, (rows, rows), 1
    )
    same = own_col_ref[...] == own_row_ref[...]
    rank_row = jnp.sum(jnp.where(earlier & same, 1, 0), axis=0, keepdims=True)
    slot_row = own_row_ref[...] * cap + rank_row
    token_row = lax.broadcasted_iota(jnp.int32, (1, rows), 1)
    seg_here = seg_ref[c]

    for r in reversed(strides):

        @pl.when(c >= r)
        def _():
            for cp in landed_copies(r):
                cp.wait_recv()

            if r < window:

                @pl.when(even)
                def _():
                    for cp in forward_copies(r, window - r - 1):
                        cp.start()

            @pl.when(jnp.logical_not(even))
            def _():
                for cp in forward_copies(r, window - r + 1):
                    cp.start()

    for r in range(1, window, 2):

        @pl.when(c >= r)
        def _():
            for cp in landed_copies(r):
                cp.wait_recv()

    block_count = window + 1
    bounds = [
        (lo, min(lo + CHUNK_BLOCKS, block_count)) for lo in range(0, block_count, CHUNK_BLOCKS)
    ]

    def attend(d):
        slots = lax.broadcasted_iota(jnp.int32, (cap, rows), 0) + d * cap
        chosen = slots == slot_row
        filled = jnp.sum(jnp.where(chosen, 1.0, 0.0), axis=1, keepdims=True)
        q_pos = jnp.sum(jnp.where(chosen, token_row, 0), axis=1, keepdims=True) + c * rows
        q_seg = jnp.sum(jnp.where(chosen, seg_here, 0), axis=1, keepdims=True)
        q_slot = jnp.dot(
            jnp.where(chosen, 1.0, 0.0).astype(jnp.bfloat16),
            q_ref[...],
            preferred_element_type=jnp.float32,
        ).astype(jnp.bfloat16)
        states = [None] * kv_local
        for lo, hi in bounds:
            width = (hi - lo) * rows
            k_seg = jnp.concatenate(
                [seg_ref[jnp.maximum(c - window + j, 0)] for j in range(lo, hi)], axis=1
            )
            k_pos = lax.broadcasted_iota(jnp.int32, (1, width), 1) + (c - window + lo) * rows
            allowed = (k_seg == q_seg) & (k_pos <= q_pos) & (k_pos >= 0)
            bias = jnp.where(allowed, 0.0, MASKED)
            for k in range(kv_local):
                head = k * HEAD_DIM
                q = jnp.concatenate(
                    [
                        q_slot[:, (k * GROUP + g) * HEAD_DIM : (k * GROUP + g + 1) * HEAD_DIM]
                        for g in range(GROUP)
                    ],
                    axis=0,
                )
                s = lax.dot_general(
                    q,
                    kbuf[lo * rows : hi * rows, head : head + HEAD_DIM],
                    (((1,), (1,)), ((), ())),
                    preferred_element_type=jnp.float32,
                )
                s = s.reshape(GROUP, cap, width) + bias[None]
                top = jnp.max(s, axis=-1, keepdims=True)
                if states[k] is not None:
                    top = jnp.maximum(top, states[k][0])
                p = jnp.exp((s - top) * scale)
                total = jnp.sum(p, axis=-1, keepdims=True)
                o = jnp.dot(
                    p.reshape(GROUP * cap, width).astype(jnp.bfloat16),
                    vbuf[lo * rows : hi * rows, head : head + HEAD_DIM],
                    preferred_element_type=jnp.float32,
                ).reshape(GROUP, cap, HEAD_DIM)
                if states[k] is not None:
                    fade = jnp.exp((states[k][0] - top) * scale)
                    total = total + states[k][1] * fade
                    o = o + states[k][2] * fade
                states[k] = (top, total, o)
        for k in range(kv_local):
            _, total, o = states[k]
            o = jnp.where(filled[None] > 0, o / total, 0.0).astype(jnp.bfloat16)
            for g in range(GROUP):
                col = (k * GROUP + g) * HEAD_DIM
                attended[d, :, col : col + HEAD_DIM] = o[g]

    def right_copy(d, t):
        return pltpu.make_async_remote_copy(
            src_ref=partial.at[d, t],
            dst_ref=landed.at[d + 1, t],
            send_sem=row_send.at[d, t],
            recv_sem=row_recv.at[d + 1, t],
            device_id={"tp": z + 1},
        )

    def left_copy(d, t):
        return pltpu.make_async_remote_copy(
            src_ref=partial.at[d, t],
            dst_ref=landed.at[d, t],
            send_sem=row_send.at[d, t],
            recv_sem=row_recv.at[d, t],
            device_id={"tp": z - 1},
        )

    def each_tile(body):
        def step(t, carry):
            body(t)
            return carry

        lax.fori_loop(0, tiles, step, 0)

    low = z < (n_tp // 2)
    first = jnp.where(low, n_tp - 1, 0)
    rest = jnp.where(low, 0, 1)
    attend(first)

    def project_first(t):
        weight_copy(t).wait()
        partial[first, t] = jnp.dot(
            attended[first], wbuf[t], preferred_element_type=jnp.float32
        ).astype(jnp.bfloat16)

        @pl.when(z == 0)
        def _():
            right_copy(n_tp - 1, t).start()

        @pl.when(z == n_tp - 1)
        def _():
            left_copy(0, t).start()

    each_tile(project_first)

    def attend_rest(i, carry):
        attend(rest + i)
        return carry

    lax.fori_loop(0, n_tp - 1, attend_rest, 0)

    def project_rest(t):
        a = attended[pl.ds(rest, n_tp - 1)].reshape((n_tp - 1) * cap, attended.shape[2])
        y = jnp.dot(a, wbuf[t], preferred_element_type=jnp.float32).astype(jnp.bfloat16)
        for i in range(n_tp - 1):
            partial[rest + i, t] = y[i * cap : (i + 1) * cap]

        @pl.when(z == 0)
        def _():
            right_copy(n_tp - 2, t).start()

        @pl.when(z == n_tp - 1)
        def _():
            left_copy(1, t).start()

    each_tile(project_rest)

    for j in range(2, n_tp - 1):

        def send_more(t):
            @pl.when(z == 0)
            def _():
                right_copy(n_tp - 1 - j, t).start()

            @pl.when(z == n_tp - 1)
            def _():
                left_copy(j, t).start()

        each_tile(send_more)

    for j in range(n_tp - 1):

        def pump(t):
            d_right = n_tp - 1 - j
            d_left = j

            @pl.when((z > 0) & (z < d_right))
            def _():
                cp = right_copy(d_right, t)
                cp.wait_recv()
                partial[d_right, t] = (
                    partial[d_right, t].astype(jnp.float32)
                    + landed[d_right + 1, t].astype(jnp.float32)
                ).astype(jnp.bfloat16)
                cp.start()

            @pl.when((z < n_tp - 1) & (z > d_left))
            def _():
                cp = left_copy(d_left, t)
                cp.wait_recv()
                partial[d_left, t] = (
                    partial[d_left, t].astype(jnp.float32)
                    + landed[d_left, t].astype(jnp.float32)
                ).astype(jnp.bfloat16)
                cp.start()

        each_tile(pump)

    def finish(t, squares):
        cols = pl.ds(pl.multiple_of(t * TILE, TILE), TILE)
        hidden[t] = res_ref[:, cols].astype(jnp.float32) + partial[z, t].astype(jnp.float32)

        @pl.when(z > 0)
        def _():
            right_copy(z, t).wait_recv()
            hidden[t] = hidden[t] + landed[z + 1, t].astype(jnp.float32)

        @pl.when(z < n_tp - 1)
        def _():
            left_copy(z, t).wait_recv()
            hidden[t] = hidden[t] + landed[z, t].astype(jnp.float32)

        h = hidden[t]
        hid_ref[:, cols] = h.astype(hid_ref.dtype)
        return squares + jnp.sum(h * h, axis=-1, keepdims=True)

    squares = lax.fori_loop(0, tiles, finish, jnp.zeros((cap, 1), jnp.float32))
    inverse = lax.rsqrt(squares / (tiles * TILE) + 1e-05)

    def scale_tile(t):
        cols = pl.ds(pl.multiple_of(t * TILE, TILE), TILE)
        norm_ref[:, cols] = (hidden[t] * inverse * gain_ref[:, cols]).astype(norm_ref.dtype)

    each_tile(scale_tile)

    for r in strides:

        @pl.when(c + r < n_ctx)
        def _():
            for cp in own_copies(r):
                cp.wait_send()

        @pl.when(c >= r)
        def _():
            if r < window:

                @pl.when(even)
                def _():
                    for cp in forward_copies(r, window - r - 1):
                        cp.wait_send()

            @pl.when(jnp.logical_not(even))
            def _():
                for cp in forward_copies(r, window - r + 1):
                    cp.wait_send()

    @pl.when(even)
    def _():
        for cp in mate_copies():
            cp.wait_send()

    for d in range(n_tp):

        def sent(t):
            @pl.when(z < d)
            def _():
                right_copy(d, t).wait_send()

            @pl.when(z > d)
            def _():
                left_copy(d, t).wait_send()

        each_tile(sent)


def on_device(n_ctx, n_tp, queries, key_rows, value_rows, segments, owner_ids, out_proj, residual, norm_gain):
    rows, width = queries.shape
    cap, model = residual.shape
    tiles = model // TILE
    keys = (n_ctx // 2 + 1) * rows
    vmem = pl.BlockSpec(memory_space=pltpu.VMEM)
    out = jax.ShapeDtypeStruct((cap, model), jnp.bfloat16)
    return pl.pallas_call(
        functools.partial(kernel, n_ctx, n_tp),
        out_shape=(out, out),
        in_specs=[vmem] * 6 + [pl.BlockSpec(memory_space=pl.ANY)] + [vmem] * 2,
        out_specs=(vmem, vmem),
        scratch_shapes=[
            pltpu.VMEM((keys, key_rows.shape[1]), jnp.bfloat16),
            pltpu.VMEM((keys, key_rows.shape[1]), jnp.bfloat16),
            pltpu.VMEM((tiles, width, TILE), jnp.bfloat16),
            pltpu.VMEM((n_tp, cap, width), jnp.bfloat16),
            pltpu.VMEM((n_tp, tiles, cap, TILE), jnp.bfloat16),
            pltpu.VMEM((n_tp + 1, tiles, cap, TILE), jnp.bfloat16),
            pltpu.VMEM((tiles, cap, TILE), jnp.float32),
            pltpu.SemaphoreType.DMA((n_ctx // 2 + 1, 2)),
            pltpu.SemaphoreType.DMA((n_ctx // 2 + 1, 2)),
            pltpu.SemaphoreType.DMA((n_ctx // 2 + 1, 2)),
            pltpu.SemaphoreType.DMA((tiles,)),
            pltpu.SemaphoreType.DMA((n_tp, tiles)),
            pltpu.SemaphoreType.DMA((n_tp + 1, tiles)),
        ],
        compiler_params=pltpu.CompilerParams(
            collective_id=0, has_side_effects=True, vmem_limit_bytes=60 * 1024 * 1024
        ),
    )(
        queries,
        key_rows,
        value_rows,
        segments.reshape(n_ctx, 1, rows),
        owner_ids,
        owner_ids.reshape(1, rows),
        out_proj,
        residual,
        norm_gain.reshape(1, model),
    )


def solution(mesh):
    placed = (
        P("ctx", "tp"),
        P("ctx", "tp"),
        P("ctx", "tp"),
        P(),
        P("ctx", None),
        P("tp", None),
        P(("ctx", "tp"), None),
        P(),
    )
    return jax.shard_map(
        functools.partial(on_device, mesh.shape["ctx"], mesh.shape["tp"]),
        mesh=mesh,
        in_specs=placed,
        out_specs=(P(("ctx", "tp"), None), P(("ctx", "tp"), None)),
        check_vma=False,
    )
```

```python
import functools
import math

import jax
import jax.numpy as jnp
from jax import lax
from jax.experimental import pallas as pl
from jax.experimental.pallas import tpu as pltpu
from jax.sharding import PartitionSpec as P

HEADS = 32
KV_HEADS = 8
HEAD_DIM = 128
GROUP = HEADS // KV_HEADS
TILE = 1024
CHUNK_BLOCKS = 5
MASKED = -1e30


def kernel(
    n_ctx,
    n_tp,
    q_ref,
    k_ref,
    v_ref,
    seg_ref,
    own_row_ref,
    w_ref,
    res_ref,
    hid_ref,
    inv_ref,
    kbuf,
    vbuf,
    wbuf,
    attended,
    partial,
    landed,
    kv_send,
    kv_fwd,
    kv_recv,
    w_sem,
    row_send,
    row_recv,
):
    c = lax.axis_index("ctx")
    z = lax.axis_index("tp")
    rows = q_ref.shape[0]
    cap = res_ref.shape[0]
    tiles = wbuf.shape[0]
    window = n_ctx // 2
    kv_local = k_ref.shape[1] // HEAD_DIM
    scale = 1.0 / math.sqrt(HEAD_DIM)
    even = c % 2 == 0
    partner = c + 1 - 2 * (c % 2)
    strides = list(range(2, window + 1, 2))

    def weight_copy(t):
        cols = pl.ds(pl.multiple_of(t * TILE, TILE), TILE)
        return pltpu.make_async_copy(w_ref.at[:, cols], wbuf.at[t], w_sem.at[t])

    for t in range(tiles):
        weight_copy(t).start()

    barrier = pltpu.get_barrier_semaphore()

    def greet(cond, where):
        @pl.when(cond)
        def _():
            pl.semaphore_signal(barrier, inc=1, device_id=where)

        return cond.astype(jnp.int32)

    expected = 1
    pl.semaphore_signal(barrier, inc=1, device_id={"ctx": partner})
    for r in strides:
        expected = expected + greet(c + r < n_ctx, {"ctx": c + r})
        expected = expected + greet(c >= r, {"ctx": c - r})
    expected = expected + greet(z + 1 < n_tp, {"tp": z + 1})
    expected = expected + greet(z > 0, {"tp": z - 1})
    pl.semaphore_wait(barrier, expected)

    def kv_copies(src, place, send, where):
        dst = pl.ds(place * rows, rows)
        out = []
        for i, (own, buf) in enumerate(((k_ref, kbuf), (v_ref, vbuf))):
            ref = own if src is None else buf.at[pl.ds(src * rows, rows)]
            out.append(
                pltpu.make_async_remote_copy(
                    src_ref=ref,
                    dst_ref=buf.at[dst],
                    send_sem=send.at[i],
                    recv_sem=kv_recv.at[place, i],
                    device_id=where,
                )
            )
        return out

    def own_copies(r):
        return kv_copies(None, window - r, kv_send.at[r], {"ctx": c + r})

    def mate_copies():
        return kv_copies(None, window - 1, kv_send.at[0], {"ctx": partner})

    def forward_copies(r, place):
        return kv_copies(window - r, place, kv_fwd.at[r], {"ctx": partner})

    def landed_copies(r):
        return kv_copies(None, window - r, kv_send.at[r], {"ctx": partner})

    for r in reversed(strides):

        @pl.when(c + r < n_ctx)
        def _():
            for cp in own_copies(r):
                cp.start()

    @pl.when(even)
    def _():
        for cp in mate_copies():
            cp.start()

    kbuf[window * rows :, :] = k_ref[...]
    vbuf[window * rows :, :] = v_ref[...]
    for r in range(1, window + 1):

        @pl.when(c < r)
        def _():
            kbuf[(window - r) * rows : (window - r + 1) * rows, :] = jnp.zeros(k_ref.shape, k_ref.dtype)
            vbuf[(window - r) * rows : (window - r + 1) * rows, :] = jnp.zeros(v_ref.shape, v_ref.dtype)

    down = lax.broadcasted_iota(jnp.int32, (rows, rows), 0)
    along = lax.broadcasted_iota(jnp.int32, (rows, rows), 1)
    own_col = jnp.sum(jnp.where(down == along, own_row_ref[...], 0), axis=1, keepdims=True)
    same = own_col == own_row_ref[...]
    rank_row = jnp.sum(jnp.where((down < along) & same, 1, 0), axis=0, keepdims=True)
    slot_row = own_row_ref[...] * cap + rank_row
    token_row = lax.broadcasted_iota(jnp.int32, (1, rows), 1)
    seg_here = seg_ref[c]

    for r in reversed(strides):

        @pl.when(c >= r)
        def _():
            for cp in landed_copies(r):
                cp.wait_recv()

            if r < window:

                @pl.when(even)
                def _():
                    for cp in forward_copies(r, window - r - 1):
                        cp.start()

            @pl.when(jnp.logical_not(even))
            def _():
                for cp in forward_copies(r, window - r + 1):
                    cp.start()

    for r in range(1, window, 2):

        @pl.when(c >= r)
        def _():
            for cp in landed_copies(r):
                cp.wait_recv()

    block_count = window + 1
    bounds = [
        (lo, min(lo + CHUNK_BLOCKS, block_count)) for lo in range(0, block_count, CHUNK_BLOCKS)
    ]

    def attend(d):
        slots = lax.broadcasted_iota(jnp.int32, (cap, rows), 0) + d * cap
        chosen = slots == slot_row
        filled = jnp.sum(jnp.where(chosen, 1.0, 0.0), axis=1, keepdims=True)
        q_pos = jnp.sum(jnp.where(chosen, token_row, 0), axis=1, keepdims=True) + c * rows
        q_seg = jnp.sum(jnp.where(chosen, seg_here, 0), axis=1, keepdims=True)
        q_slot = jnp.dot(
            jnp.where(chosen, 1.0, 0.0).astype(jnp.bfloat16),
            q_ref[...],
            preferred_element_type=jnp.float32,
        ).astype(jnp.bfloat16)
        states = [None] * kv_local
        for lo, hi in bounds:
            width = (hi - lo) * rows
            k_seg = jnp.concatenate(
                [seg_ref[jnp.maximum(c - window + j, 0)] for j in range(lo, hi)], axis=1
            )
            k_pos = lax.broadcasted_iota(jnp.int32, (1, width), 1) + (c - window + lo) * rows
            allowed = (k_seg == q_seg) & (k_pos <= q_pos) & (k_pos >= 0)
            bias = jnp.where(allowed, 0.0, MASKED)
            for k in range(kv_local):
                head = k * HEAD_DIM
                q = jnp.concatenate(
                    [
                        q_slot[:, (k * GROUP + g) * HEAD_DIM : (k * GROUP + g + 1) * HEAD_DIM]
                        for g in range(GROUP)
                    ],
                    axis=0,
                )
                s = lax.dot_general(
                    q,
                    kbuf[lo * rows : hi * rows, head : head + HEAD_DIM],
                    (((1,), (1,)), ((), ())),
                    preferred_element_type=jnp.float32,
                )
                s = s.reshape(GROUP, cap, width) + bias[None]
                top = jnp.max(s, axis=-1, keepdims=True)
                if states[k] is not None:
                    top = jnp.maximum(top, states[k][0])
                p = jnp.exp((s - top) * scale)
                total = jnp.sum(p, axis=-1, keepdims=True)
                o = jnp.dot(
                    p.reshape(GROUP * cap, width).astype(jnp.bfloat16),
                    vbuf[lo * rows : hi * rows, head : head + HEAD_DIM],
                    preferred_element_type=jnp.float32,
                ).reshape(GROUP, cap, HEAD_DIM)
                if states[k] is not None:
                    fade = jnp.exp((states[k][0] - top) * scale)
                    total = total + states[k][1] * fade
                    o = o + states[k][2] * fade
                states[k] = (top, total, o)
        for k in range(kv_local):
            _, total, o = states[k]
            o = jnp.where(filled[None] > 0, o / total, 0.0).astype(jnp.bfloat16)
            for g in range(GROUP):
                col = (k * GROUP + g) * HEAD_DIM
                attended[d, :, col : col + HEAD_DIM] = o[g]

    def right_copy(d, t):
        return pltpu.make_async_remote_copy(
            src_ref=partial.at[d, t],
            dst_ref=landed.at[d + 1, t],
            send_sem=row_send.at[d, t],
            recv_sem=row_recv.at[d + 1, t],
            device_id={"tp": z + 1},
        )

    def left_copy(d, t):
        return pltpu.make_async_remote_copy(
            src_ref=partial.at[d, t],
            dst_ref=landed.at[d, t],
            send_sem=row_send.at[d, t],
            recv_sem=row_recv.at[d, t],
            device_id={"tp": z - 1},
        )

    def each_tile(body):
        def step(t, carry):
            body(t)
            return carry

        lax.fori_loop(0, tiles, step, 0)

    low = z < (n_tp // 2)
    first = jnp.where(low, n_tp - 1, 0)
    rest = jnp.where(low, 0, 1)
    attend(first)

    def project_first(t):
        weight_copy(t).wait()
        partial[first, t] = jnp.dot(
            attended[first], wbuf[t], preferred_element_type=jnp.float32
        ).astype(jnp.bfloat16)

        @pl.when(z == 0)
        def _():
            right_copy(n_tp - 1, t).start()

        @pl.when(z == n_tp - 1)
        def _():
            left_copy(0, t).start()

    each_tile(project_first)

    def attend_rest(i, carry):
        attend(rest + i)
        return carry

    lax.fori_loop(0, n_tp - 1, attend_rest, 0)

    def project_rest(t):
        a = attended[pl.ds(rest, n_tp - 1)].reshape((n_tp - 1) * cap, attended.shape[2])
        y = jnp.dot(a, wbuf[t], preferred_element_type=jnp.float32).astype(jnp.bfloat16)
        for i in range(n_tp - 1):
            partial[rest + i, t] = y[i * cap : (i + 1) * cap]

        @pl.when(z == 0)
        def _():
            right_copy(n_tp - 2, t).start()

        @pl.when(z == n_tp - 1)
        def _():
            left_copy(1, t).start()

    each_tile(project_rest)

    for j in range(2, n_tp - 1):

        def send_more(t):
            @pl.when(z == 0)
            def _():
                right_copy(n_tp - 1 - j, t).start()

            @pl.when(z == n_tp - 1)
            def _():
                left_copy(j, t).start()

        each_tile(send_more)

    for j in range(n_tp - 1):

        def pump(t):
            d_right = n_tp - 1 - j
            d_left = j

            @pl.when((z > 0) & (z < d_right))
            def _():
                cp = right_copy(d_right, t)
                cp.wait_recv()
                partial[d_right, t] = (
                    partial[d_right, t].astype(jnp.float32)
                    + landed[d_right + 1, t].astype(jnp.float32)
                ).astype(jnp.bfloat16)
                cp.start()

            @pl.when((z < n_tp - 1) & (z > d_left))
            def _():
                cp = left_copy(d_left, t)
                cp.wait_recv()
                partial[d_left, t] = (
                    partial[d_left, t].astype(jnp.float32)
                    + landed[d_left, t].astype(jnp.float32)
                ).astype(jnp.bfloat16)
                cp.start()

        each_tile(pump)

    def finish(t, squares):
        cols = pl.ds(pl.multiple_of(t * TILE, TILE), TILE)
        hid_ref[:, cols] = res_ref[:, cols].astype(jnp.float32) + partial[z, t].astype(jnp.float32)

        @pl.when(z > 0)
        def _():
            right_copy(z, t).wait_recv()
            hid_ref[:, cols] = hid_ref[:, cols] + landed[z + 1, t].astype(jnp.float32)

        @pl.when(z < n_tp - 1)
        def _():
            left_copy(z, t).wait_recv()
            hid_ref[:, cols] = hid_ref[:, cols] + landed[z, t].astype(jnp.float32)

        h = hid_ref[:, cols]
        return squares + jnp.sum(h * h, axis=-1, keepdims=True)

    squares = lax.fori_loop(0, tiles, finish, jnp.zeros((cap, 1), jnp.float32))
    inv_ref[...] = jnp.broadcast_to(lax.rsqrt(squares / (tiles * TILE) + 1e-05), inv_ref.shape)

    for r in strides:

        @pl.when(c + r < n_ctx)
        def _():
            for cp in own_copies(r):
                cp.wait_send()

        @pl.when(c >= r)
        def _():
            if r < window:

                @pl.when(even)
                def _():
                    for cp in forward_copies(r, window - r - 1):
                        cp.wait_send()

            @pl.when(jnp.logical_not(even))
            def _():
                for cp in forward_copies(r, window - r + 1):
                    cp.wait_send()

    @pl.when(even)
    def _():
        for cp in mate_copies():
            cp.wait_send()

    for d in range(n_tp):

        def sent(t):
            @pl.when(z < d)
            def _():
                right_copy(d, t).wait_send()

            @pl.when(z > d)
            def _():
                left_copy(d, t).wait_send()

        each_tile(sent)


def on_device(n_ctx, n_tp, queries, key_rows, value_rows, segments, owner_ids, out_proj, residual, norm_gain):
    rows, width = queries.shape
    cap, model = residual.shape
    tiles = model // TILE
    keys = (n_ctx // 2 + 1) * rows
    vmem = pl.BlockSpec(memory_space=pltpu.VMEM)
    hidden, inverse = pl.pallas_call(
        functools.partial(kernel, n_ctx, n_tp),
        out_shape=(
            jax.ShapeDtypeStruct((cap, model), jnp.float32),
            jax.ShapeDtypeStruct((cap, HEAD_DIM), jnp.float32),
        ),
        in_specs=[vmem] * 5 + [pl.BlockSpec(memory_space=pl.ANY), vmem],
        out_specs=(vmem, vmem),
        scratch_shapes=[
            pltpu.VMEM((keys, key_rows.shape[1]), jnp.bfloat16),
            pltpu.VMEM((keys, key_rows.shape[1]), jnp.bfloat16),
            pltpu.VMEM((tiles, width, TILE), jnp.bfloat16),
            pltpu.VMEM((n_tp, cap, width), jnp.bfloat16),
            pltpu.VMEM((n_tp, tiles, cap, TILE), jnp.bfloat16),
            pltpu.VMEM((n_tp + 1, tiles, cap, TILE), jnp.bfloat16),
            pltpu.SemaphoreType.DMA((n_ctx // 2 + 1, 2)),
            pltpu.SemaphoreType.DMA((n_ctx // 2 + 1, 2)),
            pltpu.SemaphoreType.DMA((n_ctx // 2 + 1, 2)),
            pltpu.SemaphoreType.DMA((tiles,)),
            pltpu.SemaphoreType.DMA((n_tp, tiles)),
            pltpu.SemaphoreType.DMA((n_tp + 1, tiles)),
        ],
        compiler_params=pltpu.CompilerParams(
            collective_id=0, has_side_effects=True, vmem_limit_bytes=60 * 1024 * 1024
        ),
    )(
        queries,
        key_rows,
        value_rows,
        segments.reshape(n_ctx, 1, rows),
        owner_ids.reshape(1, rows),
        out_proj,
        residual,
    )
    normed = hidden * inverse[:, :1] * norm_gain
    return (hidden.astype(jnp.bfloat16), normed.astype(jnp.bfloat16))


def solution(mesh):
    placed = (
        P("ctx", "tp"),
        P("ctx", "tp"),
        P("ctx", "tp"),
        P(),
        P("ctx", None),
        P("tp", None),
        P(("ctx", "tp"), None),
        P(),
    )
    return jax.shard_map(
        functools.partial(on_device, mesh.shape["ctx"], mesh.shape["tp"]),
        mesh=mesh,
        in_specs=placed,
        out_specs=(P(("ctx", "tp"), None), P(("ctx", "tp"), None)),
        check_vma=False,
    )
```

```python
import functools
import math

import jax
import jax.numpy as jnp
from jax import lax
from jax.experimental import pallas as pl
from jax.experimental.pallas import tpu as pltpu
from jax.sharding import PartitionSpec as P

HEADS = 32
KV_HEADS = 8
HEAD_DIM = 128
GROUP = HEADS // KV_HEADS
TILE = 1024
CHUNK_BLOCKS = 5
FAR_TILES = 2
MASKED = -1e30


def kernel(
    n_ctx,
    n_tp,
    q_ref,
    k_ref,
    v_ref,
    seg_ref,
    own_row_ref,
    w_ref,
    res_ref,
    hid_ref,
    inv_ref,
    kbuf,
    vbuf,
    wbuf,
    attended,
    partial,
    landed,
    wfar,
    attfar,
    kv_send,
    kv_fwd,
    kv_recv,
    w_sem,
    row_send,
    row_recv,
    ship_send,
    spread_send,
    spread_recv,
    far_send,
    far_recv,
):
    c = lax.axis_index("ctx")
    z = lax.axis_index("tp")
    rows = q_ref.shape[0]
    cap = res_ref.shape[0]
    tiles = wbuf.shape[0]
    window = n_ctx // 2
    kv_local = k_ref.shape[1] // HEAD_DIM
    scale = 1.0 / math.sqrt(HEAD_DIM)
    even = c % 2 == 0
    partner = c + 1 - 2 * (c % 2)
    strides = list(range(2, window + 1, 2))

    def weight_copy(t):
        cols = pl.ds(pl.multiple_of(t * TILE, TILE), TILE)
        return pltpu.make_async_copy(w_ref.at[:, cols], wbuf.at[t], w_sem.at[t])

    for t in range(tiles):
        weight_copy(t).start()

    barrier = pltpu.get_barrier_semaphore()

    def greet(cond, where):
        @pl.when(cond)
        def _():
            pl.semaphore_signal(barrier, inc=1, device_id=where)

        return cond.astype(jnp.int32)

    expected = 1
    pl.semaphore_signal(barrier, inc=1, device_id={"ctx": partner})
    for r in range(2, n_ctx, 2):
        pl.semaphore_signal(barrier, inc=1, device_id={"ctx": (c + r) % n_ctx})
        expected = expected + 1
    expected = expected + greet(z + 1 < n_tp, {"tp": z + 1})
    expected = expected + greet(z > 0, {"tp": z - 1})
    pl.semaphore_wait(barrier, expected)

    near = tiles - FAR_TILES
    at_end = (z == 0) | (z == n_tp - 1)
    helper = (z == 1) | (z == n_tp - 2)
    inward = jnp.where(z == 0, 1, n_tp - 2)
    share = w_ref.shape[0] // n_ctx

    def w_rows(who):
        return pl.ds(pl.multiple_of(who * share, share), share)

    def ship_copy(f):
        return pltpu.make_async_remote_copy(
            src_ref=w_ref.at[w_rows(c), pl.ds((near + f) * TILE, TILE)],
            dst_ref=wfar.at[f, w_rows(c)],
            send_sem=ship_send.at[f],
            recv_sem=spread_recv.at[0, f],
            device_id={"tp": inward},
        )

    def spread_copy(r, f):
        return pltpu.make_async_remote_copy(
            src_ref=wfar.at[f, w_rows(c)],
            dst_ref=wfar.at[f, w_rows(c)],
            send_sem=spread_send.at[r, f],
            recv_sem=spread_recv.at[r, f],
            device_id={"ctx": (c + r) % n_ctx},
        )

    def mate_weights(r, f):
        slice_rows = w_rows((c - r + n_ctx) % n_ctx)
        return pltpu.make_async_remote_copy(
            src_ref=wfar.at[f, slice_rows],
            dst_ref=wfar.at[f, slice_rows],
            send_sem=spread_send.at[r + 1, f],
            recv_sem=spread_recv.at[(r + 2 - 2 * (c % 2) - 1 + n_ctx) % n_ctx, f],
            device_id={"ctx": partner},
        )

    def far_copy(d):
        return pltpu.make_async_remote_copy(
            src_ref=attended.at[d],
            dst_ref=attfar.at[d],
            send_sem=far_send.at[d],
            recv_sem=far_recv.at[d],
            device_id={"tp": inward},
        )

    @pl.when(at_end)
    def _():
        for f in range(FAR_TILES):
            ship_copy(f).start()

    def kv_copies(src, place, send, where):
        dst = pl.ds(place * rows, rows)
        out = []
        for i, (own, buf) in enumerate(((k_ref, kbuf), (v_ref, vbuf))):
            ref = own if src is None else buf.at[pl.ds(src * rows, rows)]
            out.append(
                pltpu.make_async_remote_copy(
                    src_ref=ref,
                    dst_ref=buf.at[dst],
                    send_sem=send.at[i],
                    recv_sem=kv_recv.at[place, i],
                    device_id=where,
                )
            )
        return out

    def own_copies(r):
        return kv_copies(None, window - r, kv_send.at[r], {"ctx": c + r})

    def mate_copies():
        return kv_copies(None, window - 1, kv_send.at[0], {"ctx": partner})

    def forward_copies(r, place):
        return kv_copies(window - r, place, kv_fwd.at[r], {"ctx": partner})

    def landed_copies(r):
        return kv_copies(None, window - r, kv_send.at[r], {"ctx": partner})

    for r in reversed(strides):

        @pl.when(c + r < n_ctx)
        def _():
            for cp in own_copies(r):
                cp.start()

    @pl.when(even)
    def _():
        for cp in mate_copies():
            cp.start()

    kbuf[window * rows :, :] = k_ref[...]
    vbuf[window * rows :, :] = v_ref[...]
    for r in range(1, window + 1):

        @pl.when(c < r)
        def _():
            kbuf[(window - r) * rows : (window - r + 1) * rows, :] = jnp.zeros(k_ref.shape, k_ref.dtype)
            vbuf[(window - r) * rows : (window - r + 1) * rows, :] = jnp.zeros(v_ref.shape, v_ref.dtype)

    down = lax.broadcasted_iota(jnp.int32, (rows, rows), 0)
    along = lax.broadcasted_iota(jnp.int32, (rows, rows), 1)
    own_col = jnp.sum(jnp.where(down == along, own_row_ref[...], 0), axis=1, keepdims=True)
    same = own_col == own_row_ref[...]
    rank_row = jnp.sum(jnp.where((down < along) & same, 1, 0), axis=0, keepdims=True)
    slot_row = own_row_ref[...] * cap + rank_row
    token_row = lax.broadcasted_iota(jnp.int32, (1, rows), 1)
    seg_here = seg_ref[c]

    for r in reversed(strides):

        @pl.when(c >= r)
        def _():
            for cp in landed_copies(r):
                cp.wait_recv()

            if r < window:

                @pl.when(even)
                def _():
                    for cp in forward_copies(r, window - r - 1):
                        cp.start()

            @pl.when(jnp.logical_not(even))
            def _():
                for cp in forward_copies(r, window - r + 1):
                    cp.start()

    for r in range(1, window, 2):

        @pl.when(c >= r)
        def _():
            for cp in landed_copies(r):
                cp.wait_recv()

    block_count = window + 1
    bounds = [
        (lo, min(lo + CHUNK_BLOCKS, block_count)) for lo in range(0, block_count, CHUNK_BLOCKS)
    ]

    def attend(d):
        slots = lax.broadcasted_iota(jnp.int32, (cap, rows), 0) + d * cap
        chosen = slots == slot_row
        filled = jnp.sum(jnp.where(chosen, 1.0, 0.0), axis=1, keepdims=True)
        q_pos = jnp.sum(jnp.where(chosen, token_row, 0), axis=1, keepdims=True) + c * rows
        q_seg = jnp.sum(jnp.where(chosen, seg_here, 0), axis=1, keepdims=True)
        q_slot = jnp.dot(
            jnp.where(chosen, 1.0, 0.0).astype(jnp.bfloat16),
            q_ref[...],
            preferred_element_type=jnp.float32,
        ).astype(jnp.bfloat16)
        states = [None] * kv_local
        for lo, hi in bounds:
            width = (hi - lo) * rows
            k_seg = jnp.concatenate(
                [seg_ref[jnp.maximum(c - window + j, 0)] for j in range(lo, hi)], axis=1
            )
            k_pos = lax.broadcasted_iota(jnp.int32, (1, width), 1) + (c - window + lo) * rows
            allowed = (k_seg == q_seg) & (k_pos <= q_pos) & (k_pos >= 0)
            bias = jnp.where(allowed, 0.0, MASKED)
            for k in range(kv_local):
                head = k * HEAD_DIM
                q = jnp.concatenate(
                    [
                        q_slot[:, (k * GROUP + g) * HEAD_DIM : (k * GROUP + g + 1) * HEAD_DIM]
                        for g in range(GROUP)
                    ],
                    axis=0,
                )
                s = lax.dot_general(
                    q,
                    kbuf[lo * rows : hi * rows, head : head + HEAD_DIM],
                    (((1,), (1,)), ((), ())),
                    preferred_element_type=jnp.float32,
                )
                s = s.reshape(GROUP, cap, width) + bias[None]
                top = jnp.max(s, axis=-1, keepdims=True)
                if states[k] is not None:
                    top = jnp.maximum(top, states[k][0])
                p = jnp.exp((s - top) * scale)
                total = jnp.sum(p, axis=-1, keepdims=True)
                o = jnp.dot(
                    p.reshape(GROUP * cap, width).astype(jnp.bfloat16),
                    vbuf[lo * rows : hi * rows, head : head + HEAD_DIM],
                    preferred_element_type=jnp.float32,
                ).reshape(GROUP, cap, HEAD_DIM)
                if states[k] is not None:
                    fade = jnp.exp((states[k][0] - top) * scale)
                    total = total + states[k][1] * fade
                    o = o + states[k][2] * fade
                states[k] = (top, total, o)
        for k in range(kv_local):
            _, total, o = states[k]
            o = jnp.where(filled[None] > 0, o / total, 0.0).astype(jnp.bfloat16)
            for g in range(GROUP):
                col = (k * GROUP + g) * HEAD_DIM
                attended[d, :, col : col + HEAD_DIM] = o[g]

    def right_copy(d, t):
        return pltpu.make_async_remote_copy(
            src_ref=partial.at[d, t],
            dst_ref=landed.at[d + 1, t],
            send_sem=row_send.at[d, t],
            recv_sem=row_recv.at[d + 1, t],
            device_id={"tp": z + 1},
        )

    def left_copy(d, t):
        return pltpu.make_async_remote_copy(
            src_ref=partial.at[d, t],
            dst_ref=landed.at[d, t],
            send_sem=row_send.at[d, t],
            recv_sem=row_recv.at[d, t],
            device_id={"tp": z - 1},
        )

    def each_tile(body, start=0, stop=tiles):
        def step(t, carry):
            body(t)
            return carry

        lax.fori_loop(start, stop, step, 0)

    low = z < (n_tp // 2)
    first = jnp.where(low, n_tp - 1, 0)
    rest = jnp.where(low, 0, 1)

    @pl.when(helper)
    def _():
        for f in range(FAR_TILES):
            spread_copy(0, f).wait_recv()
            for r in range(2, n_ctx, 2):
                spread_copy(r, f).start()
            mate_weights(0, f).start()

    attend(first)

    def project_first(t):
        weight_copy(t).wait()
        partial[first, t] = jnp.dot(
            attended[first], wbuf[t], preferred_element_type=jnp.float32
        ).astype(jnp.bfloat16)

        @pl.when((z == 0) & (t < near))
        def _():
            right_copy(n_tp - 1, t).start()

        @pl.when((z == n_tp - 1) & (t < near))
        def _():
            left_copy(0, t).start()

    each_tile(project_first)

    def attend_rest(i, carry):
        attend(rest + i)
        return carry

    lax.fori_loop(0, n_tp - 1, attend_rest, 0)

    @pl.when(at_end)
    def _():
        for i in range(n_tp - 1):
            far_copy(jnp.where(z == 0, n_tp - 1 - i, i)).start()

    def project_rest(t):
        a = attended[pl.ds(rest, n_tp - 1)].reshape((n_tp - 1) * cap, attended.shape[2])
        y = jnp.dot(a, wbuf[t], preferred_element_type=jnp.float32).astype(jnp.bfloat16)
        for i in range(n_tp - 1):
            partial[rest + i, t] = y[i * cap : (i + 1) * cap]

        @pl.when((z == 0) & (t < near))
        def _():
            right_copy(n_tp - 2, t).start()

        @pl.when((z == n_tp - 1) & (t < near))
        def _():
            left_copy(1, t).start()

    each_tile(project_rest)

    for j in range(2, n_tp - 1):

        def send_more(t):
            @pl.when(z == 0)
            def _():
                right_copy(n_tp - 1 - j, t).start()

            @pl.when(z == n_tp - 1)
            def _():
                left_copy(j, t).start()

        each_tile(send_more, 0, near)

    def pump(j, t):
        d_right = n_tp - 1 - j
        d_left = j

        @pl.when((z > 0) & (z < d_right) & ((t < near) | (z > 1)))
        def _():
            cp = right_copy(d_right, t)
            cp.wait_recv()
            partial[d_right, t] = (
                partial[d_right, t].astype(jnp.float32)
                + landed[d_right + 1, t].astype(jnp.float32)
            ).astype(jnp.bfloat16)
            cp.start()

        @pl.when((z < n_tp - 1) & (z > d_left) & ((t < near) | (z < n_tp - 2)))
        def _():
            cp = left_copy(d_left, t)
            cp.wait_recv()
            partial[d_left, t] = (
                partial[d_left, t].astype(jnp.float32)
                + landed[d_left, t].astype(jnp.float32)
            ).astype(jnp.bfloat16)
            cp.start()

    @pl.when(helper)
    def _():
        for f in range(FAR_TILES):
            for r in range(2, n_ctx, 2):
                spread_copy(r, f).wait_recv()
                mate_weights(r, f).start()

    each_tile(functools.partial(pump, 0), 0, near)

    @pl.when(helper)
    def _():
        base = jnp.where(z == 1, 1, 0)
        for f in range(FAR_TILES):
            for r in range(1, n_ctx, 2):
                spread_copy(r, f).wait_recv()
        for i in range(n_tp - 1):
            far_copy(base + i).wait_recv()

        def far_tile(t):
            a = attfar[pl.ds(base, n_tp - 1)].reshape((n_tp - 1) * cap, attended.shape[2])
            y = jnp.dot(a, wfar[t - near], preferred_element_type=jnp.float32)
            for i in range(n_tp - 1):
                d = base + i
                partial[d, t] = (
                    partial[d, t].astype(jnp.float32) + y[i * cap : (i + 1) * cap]
                ).astype(jnp.bfloat16)

        each_tile(far_tile, near, tiles)

        for j in range(n_tp - 2):

            def far_send_on(t):
                @pl.when(z == 1)
                def _():
                    right_copy(n_tp - 1 - j, t).start()

                @pl.when(z == n_tp - 2)
                def _():
                    left_copy(j, t).start()

            each_tile(far_send_on, near, tiles)

    for j in range(1, n_tp - 1):
        each_tile(functools.partial(pump, j), 0, near)
    for j in range(n_tp - 1):
        each_tile(functools.partial(pump, j), near, tiles)

    def finish(t, squares):
        cols = pl.ds(pl.multiple_of(t * TILE, TILE), TILE)
        hid_ref[:, cols] = res_ref[:, cols].astype(jnp.float32) + partial[z, t].astype(jnp.float32)

        @pl.when((z > 0) & ((t < near) | (z > 1)))
        def _():
            right_copy(z, t).wait_recv()
            hid_ref[:, cols] = hid_ref[:, cols] + landed[z + 1, t].astype(jnp.float32)

        @pl.when((z < n_tp - 1) & ((t < near) | (z < n_tp - 2)))
        def _():
            left_copy(z, t).wait_recv()
            hid_ref[:, cols] = hid_ref[:, cols] + landed[z, t].astype(jnp.float32)

        h = hid_ref[:, cols]
        return squares + jnp.sum(h * h, axis=-1, keepdims=True)

    squares = lax.fori_loop(0, tiles, finish, jnp.zeros((cap, 1), jnp.float32))
    inv_ref[...] = jnp.broadcast_to(lax.rsqrt(squares / (tiles * TILE) + 1e-05), inv_ref.shape)

    for r in strides:

        @pl.when(c + r < n_ctx)
        def _():
            for cp in own_copies(r):
                cp.wait_send()

        @pl.when(c >= r)
        def _():
            if r < window:

                @pl.when(even)
                def _():
                    for cp in forward_copies(r, window - r - 1):
                        cp.wait_send()

            @pl.when(jnp.logical_not(even))
            def _():
                for cp in forward_copies(r, window - r + 1):
                    cp.wait_send()

    @pl.when(even)
    def _():
        for cp in mate_copies():
            cp.wait_send()

    for d in range(n_tp):

        def sent(t):
            @pl.when((z < d) & ((t < near) | (z > 0)))
            def _():
                right_copy(d, t).wait_send()

            @pl.when((z > d) & ((t < near) | (z < n_tp - 1)))
            def _():
                left_copy(d, t).wait_send()

        each_tile(sent)

    @pl.when(at_end)
    def _():
        for f in range(FAR_TILES):
            ship_copy(f).wait_send()
        for i in range(n_tp - 1):
            far_copy(jnp.where(z == 0, n_tp - 1 - i, i)).wait_send()

    @pl.when(helper)
    def _():
        for f in range(FAR_TILES):
            mate_weights(0, f).wait_send()
            for r in range(2, n_ctx, 2):
                spread_copy(r, f).wait_send()
                mate_weights(r, f).wait_send()


def scale_rows(hidden_ref, inverse_ref, gain_ref, hid_ref, norm_ref):
    h = hidden_ref[...]
    hid_ref[...] = h.astype(hid_ref.dtype)
    norm_ref[...] = (h * inverse_ref[:, :1] * gain_ref[...]).astype(norm_ref.dtype)


def on_device(n_ctx, n_tp, queries, key_rows, value_rows, segments, owner_ids, out_proj, residual, norm_gain):
    rows, width = queries.shape
    cap, model = residual.shape
    tiles = model // TILE
    keys = (n_ctx // 2 + 1) * rows
    vmem = pl.BlockSpec(memory_space=pltpu.VMEM)
    hidden, inverse = pl.pallas_call(
        functools.partial(kernel, n_ctx, n_tp),
        out_shape=(
            jax.ShapeDtypeStruct((cap, model), jnp.float32),
            jax.ShapeDtypeStruct((cap, HEAD_DIM), jnp.float32),
        ),
        in_specs=[vmem] * 5 + [pl.BlockSpec(memory_space=pl.ANY), vmem],
        out_specs=(vmem, vmem),
        scratch_shapes=[
            pltpu.VMEM((keys, key_rows.shape[1]), jnp.bfloat16),
            pltpu.VMEM((keys, key_rows.shape[1]), jnp.bfloat16),
            pltpu.VMEM((tiles, width, TILE), jnp.bfloat16),
            pltpu.VMEM((n_tp, cap, width), jnp.bfloat16),
            pltpu.VMEM((n_tp, tiles, cap, TILE), jnp.bfloat16),
            pltpu.VMEM((n_tp + 1, tiles, cap, TILE), jnp.bfloat16),
            pltpu.VMEM((FAR_TILES, width, TILE), jnp.bfloat16),
            pltpu.VMEM((n_tp, cap, width), jnp.bfloat16),
            pltpu.SemaphoreType.DMA((n_ctx // 2 + 1, 2)),
            pltpu.SemaphoreType.DMA((n_ctx // 2 + 1, 2)),
            pltpu.SemaphoreType.DMA((n_ctx // 2 + 1, 2)),
            pltpu.SemaphoreType.DMA((tiles,)),
            pltpu.SemaphoreType.DMA((n_tp, tiles)),
            pltpu.SemaphoreType.DMA((n_tp + 1, tiles)),
            pltpu.SemaphoreType.DMA((FAR_TILES,)),
            pltpu.SemaphoreType.DMA((n_ctx, FAR_TILES)),
            pltpu.SemaphoreType.DMA((n_ctx, FAR_TILES)),
            pltpu.SemaphoreType.DMA((n_tp,)),
            pltpu.SemaphoreType.DMA((n_tp,)),
        ],
        compiler_params=pltpu.CompilerParams(
            collective_id=0, has_side_effects=True, vmem_limit_bytes=60 * 1024 * 1024
        ),
    )(
        queries,
        key_rows,
        value_rows,
        segments.reshape(n_ctx, 1, rows),
        owner_ids.reshape(1, rows),
        out_proj,
        residual,
    )
    out = jax.ShapeDtypeStruct((cap, model), jnp.bfloat16)
    part = pl.BlockSpec((16, model), lambda i: (i, 0))
    return pl.pallas_call(
        scale_rows,
        grid=(cap // 16,),
        out_shape=(out, out),
        in_specs=[
            part,
            pl.BlockSpec((16, HEAD_DIM), lambda i: (i, 0)),
            pl.BlockSpec((1, model), lambda i: (0, 0)),
        ],
        out_specs=(part, part),
    )(hidden, inverse, norm_gain.reshape(1, model))


def solution(mesh):
    placed = (
        P("ctx", "tp"),
        P("ctx", "tp"),
        P("ctx", "tp"),
        P(),
        P("ctx", None),
        P("tp", None),
        P(("ctx", "tp"), None),
        P(),
    )
    return jax.shard_map(
        functools.partial(on_device, mesh.shape["ctx"], mesh.shape["tp"]),
        mesh=mesh,
        in_specs=placed,
        out_specs=(P(("ctx", "tp"), None), P(("ctx", "tp"), None)),
        check_vma=False,
    )
```

```python
import functools
import math

import jax
import jax.numpy as jnp
from jax import lax
from jax.experimental import pallas as pl
from jax.experimental.pallas import tpu as pltpu
from jax.sharding import PartitionSpec as P

HEADS = 32
KV_HEADS = 8
HEAD_DIM = 128
GROUP = HEADS // KV_HEADS
TILE = 1024
CHUNK_BLOCKS = 5
FAR_TILES = 2
MASKED = -1e30


def kernel(
    n_ctx,
    n_tp,
    q_ref,
    k_ref,
    v_ref,
    seg_ref,
    own_row_ref,
    w_ref,
    res_ref,
    hid_ref,
    inv_ref,
    kbuf,
    vbuf,
    wbuf,
    attended,
    partial,
    landed,
    wfar,
    attfar,
    kv_send,
    kv_fwd,
    kv_recv,
    w_sem,
    row_send,
    row_recv,
    ship_send,
    spread_send,
    spread_recv,
    far_send,
    far_recv,
):
    c = lax.axis_index("ctx")
    z = lax.axis_index("tp")
    rows = q_ref.shape[0]
    cap = res_ref.shape[0]
    tiles = wbuf.shape[0]
    window = n_ctx // 2
    kv_local = k_ref.shape[1] // HEAD_DIM
    scale = 1.0 / math.sqrt(HEAD_DIM)
    even = c % 2 == 0
    partner = c + 1 - 2 * (c % 2)
    strides = list(range(2, window + 1, 2))

    def weight_copy(t):
        cols = pl.ds(pl.multiple_of(t * TILE, TILE), TILE)
        return pltpu.make_async_copy(w_ref.at[:, cols], wbuf.at[t], w_sem.at[t])

    for t in range(tiles):
        weight_copy(t).start()

    barrier = pltpu.get_barrier_semaphore()

    def greet(cond, where):
        @pl.when(cond)
        def _():
            pl.semaphore_signal(barrier, inc=1, device_id=where)

        return cond.astype(jnp.int32)

    expected = 1
    pl.semaphore_signal(barrier, inc=1, device_id={"ctx": partner})
    for r in range(2, n_ctx, 2):
        pl.semaphore_signal(barrier, inc=1, device_id={"ctx": (c + r) % n_ctx})
        expected = expected + 1
    expected = expected + greet(z + 1 < n_tp, {"tp": z + 1})
    expected = expected + greet(z > 0, {"tp": z - 1})
    pl.semaphore_wait(barrier, expected)

    near = tiles - FAR_TILES
    at_end = (z == 0) | (z == n_tp - 1)
    helper = (z == 1) | (z == n_tp - 2)
    inward = jnp.where(z == 0, 1, n_tp - 2)
    share = w_ref.shape[0] // n_ctx

    def w_rows(who):
        return pl.ds(pl.multiple_of(who * share, share), share)

    def ship_copy(f):
        return pltpu.make_async_remote_copy(
            src_ref=w_ref.at[w_rows(c), pl.ds((near + f) * TILE, TILE)],
            dst_ref=wfar.at[f, w_rows(c)],
            send_sem=ship_send.at[f],
            recv_sem=spread_recv.at[0, f],
            device_id={"tp": inward},
        )

    def spread_copy(r, f):
        return pltpu.make_async_remote_copy(
            src_ref=wfar.at[f, w_rows(c)],
            dst_ref=wfar.at[f, w_rows(c)],
            send_sem=spread_send.at[r, f],
            recv_sem=spread_recv.at[r, f],
            device_id={"ctx": (c + r) % n_ctx},
        )

    def mate_weights(r, f):
        slice_rows = w_rows((c - r + n_ctx) % n_ctx)
        return pltpu.make_async_remote_copy(
            src_ref=wfar.at[f, slice_rows],
            dst_ref=wfar.at[f, slice_rows],
            send_sem=spread_send.at[r + 1, f],
            recv_sem=spread_recv.at[(r + 2 - 2 * (c % 2) - 1 + n_ctx) % n_ctx, f],
            device_id={"ctx": partner},
        )

    def far_copy(d):
        return pltpu.make_async_remote_copy(
            src_ref=attended.at[d],
            dst_ref=attfar.at[d],
            send_sem=far_send.at[d],
            recv_sem=far_recv.at[d],
            device_id={"tp": inward},
        )

    def kv_copies(src, place, send, where):
        dst = pl.ds(place * rows, rows)
        out = []
        for i, (own, buf) in enumerate(((k_ref, kbuf), (v_ref, vbuf))):
            ref = own if src is None else buf.at[pl.ds(src * rows, rows)]
            out.append(
                pltpu.make_async_remote_copy(
                    src_ref=ref,
                    dst_ref=buf.at[dst],
                    send_sem=send.at[i],
                    recv_sem=kv_recv.at[place, i],
                    device_id=where,
                )
            )
        return out

    def own_copies(r):
        return kv_copies(None, window - r, kv_send.at[r], {"ctx": c + r})

    def mate_copies():
        return kv_copies(None, window - 1, kv_send.at[0], {"ctx": partner})

    def forward_copies(r, place):
        return kv_copies(window - r, place, kv_fwd.at[r], {"ctx": partner})

    def landed_copies(r):
        return kv_copies(None, window - r, kv_send.at[r], {"ctx": partner})

    for r in reversed(strides):

        @pl.when(c + r < n_ctx)
        def _():
            for cp in own_copies(r):
                cp.start()

    @pl.when(even)
    def _():
        for cp in mate_copies():
            cp.start()

    @pl.when(at_end)
    def _():
        for f in range(FAR_TILES):
            ship_copy(f).start()

    kbuf[window * rows :, :] = k_ref[...]
    vbuf[window * rows :, :] = v_ref[...]
    for r in range(1, window + 1):

        @pl.when(c < r)
        def _():
            kbuf[(window - r) * rows : (window - r + 1) * rows, :] = jnp.zeros(k_ref.shape, k_ref.dtype)
            vbuf[(window - r) * rows : (window - r + 1) * rows, :] = jnp.zeros(v_ref.shape, v_ref.dtype)

    down = lax.broadcasted_iota(jnp.int32, (rows, rows), 0)
    along = lax.broadcasted_iota(jnp.int32, (rows, rows), 1)
    own_col = jnp.sum(jnp.where(down == along, own_row_ref[...], 0), axis=1, keepdims=True)
    same = own_col == own_row_ref[...]
    rank_row = jnp.sum(jnp.where((down < along) & same, 1, 0), axis=0, keepdims=True)
    slot_row = own_row_ref[...] * cap + rank_row
    token_row = lax.broadcasted_iota(jnp.int32, (1, rows), 1)
    seg_here = seg_ref[c]

    for r in reversed(strides):

        @pl.when(c >= r)
        def _():
            for cp in landed_copies(r):
                cp.wait_recv()

            if r < window:

                @pl.when(even)
                def _():
                    for cp in forward_copies(r, window - r - 1):
                        cp.start()

            @pl.when(jnp.logical_not(even))
            def _():
                for cp in forward_copies(r, window - r + 1):
                    cp.start()

    for r in range(1, window, 2):

        @pl.when(c >= r)
        def _():
            for cp in landed_copies(r):
                cp.wait_recv()

    block_count = window + 1
    bounds = [
        (lo, min(lo + CHUNK_BLOCKS, block_count)) for lo in range(0, block_count, CHUNK_BLOCKS)
    ]

    def attend(d):
        slots = lax.broadcasted_iota(jnp.int32, (cap, rows), 0) + d * cap
        chosen = slots == slot_row
        filled = jnp.sum(jnp.where(chosen, 1.0, 0.0), axis=1, keepdims=True)
        q_pos = jnp.sum(jnp.where(chosen, token_row, 0), axis=1, keepdims=True) + c * rows
        q_seg = jnp.sum(jnp.where(chosen, seg_here, 0), axis=1, keepdims=True)
        q_slot = jnp.dot(
            jnp.where(chosen, 1.0, 0.0).astype(jnp.bfloat16),
            q_ref[...],
            preferred_element_type=jnp.float32,
        ).astype(jnp.bfloat16)
        states = [None] * kv_local
        for lo, hi in bounds:
            width = (hi - lo) * rows
            k_seg = jnp.concatenate(
                [seg_ref[jnp.maximum(c - window + j, 0)] for j in range(lo, hi)], axis=1
            )
            k_pos = lax.broadcasted_iota(jnp.int32, (1, width), 1) + (c - window + lo) * rows
            allowed = (k_seg == q_seg) & (k_pos <= q_pos) & (k_pos >= 0)
            bias = jnp.where(allowed, 0.0, MASKED)
            for k in range(kv_local):
                head = k * HEAD_DIM
                q = jnp.concatenate(
                    [
                        q_slot[:, (k * GROUP + g) * HEAD_DIM : (k * GROUP + g + 1) * HEAD_DIM]
                        for g in range(GROUP)
                    ],
                    axis=0,
                )
                s = lax.dot_general(
                    q,
                    kbuf[lo * rows : hi * rows, head : head + HEAD_DIM],
                    (((1,), (1,)), ((), ())),
                    preferred_element_type=jnp.float32,
                )
                s = s.reshape(GROUP, cap, width) + bias[None]
                top = jnp.max(s, axis=-1, keepdims=True)
                if states[k] is not None:
                    top = jnp.maximum(top, states[k][0])
                p = jnp.exp((s - top) * scale)
                total = jnp.sum(p, axis=-1, keepdims=True)
                o = jnp.dot(
                    p.reshape(GROUP * cap, width).astype(jnp.bfloat16),
                    vbuf[lo * rows : hi * rows, head : head + HEAD_DIM],
                    preferred_element_type=jnp.float32,
                ).reshape(GROUP, cap, HEAD_DIM)
                if states[k] is not None:
                    fade = jnp.exp((states[k][0] - top) * scale)
                    total = total + states[k][1] * fade
                    o = o + states[k][2] * fade
                states[k] = (top, total, o)
        for k in range(kv_local):
            _, total, o = states[k]
            o = jnp.where(filled[None] > 0, o / total, 0.0).astype(jnp.bfloat16)
            for g in range(GROUP):
                col = (k * GROUP + g) * HEAD_DIM
                attended[d, :, col : col + HEAD_DIM] = o[g]

    def right_copy(d, t):
        return pltpu.make_async_remote_copy(
            src_ref=partial.at[d, t],
            dst_ref=landed.at[d + 1, t],
            send_sem=row_send.at[d, t],
            recv_sem=row_recv.at[d + 1, t],
            device_id={"tp": z + 1},
        )

    def left_copy(d, t):
        return pltpu.make_async_remote_copy(
            src_ref=partial.at[d, t],
            dst_ref=landed.at[d, t],
            send_sem=row_send.at[d, t],
            recv_sem=row_recv.at[d, t],
            device_id={"tp": z - 1},
        )

    def each_tile(body, start=0, stop=tiles):
        def step(t, carry):
            body(t)
            return carry

        lax.fori_loop(start, stop, step, 0)

    low = z < (n_tp // 2)
    first = jnp.where(low, n_tp - 1, 0)
    rest = jnp.where(low, 0, 1)

    @pl.when(helper)
    def _():
        for f in range(FAR_TILES):
            spread_copy(0, f).wait_recv()
            for r in range(2, n_ctx, 2):
                spread_copy(r, f).start()
            mate_weights(0, f).start()

    attend(first)

    def project_first(t):
        weight_copy(t).wait()
        partial[first, t] = jnp.dot(
            attended[first], wbuf[t], preferred_element_type=jnp.float32
        ).astype(jnp.bfloat16)

        @pl.when((z == 0) & (t < near))
        def _():
            right_copy(n_tp - 1, t).start()

        @pl.when((z == n_tp - 1) & (t < near))
        def _():
            left_copy(0, t).start()

    each_tile(project_first)

    def attend_rest(i, carry):
        attend(rest + i)
        return carry

    lax.fori_loop(0, n_tp - 1, attend_rest, 0)

    @pl.when(at_end)
    def _():
        for i in range(n_tp - 1):
            far_copy(jnp.where(z == 0, n_tp - 1 - i, i)).start()

    def project_rest(t):
        a = attended[pl.ds(rest, n_tp - 1)].reshape((n_tp - 1) * cap, attended.shape[2])
        y = jnp.dot(a, wbuf[t], preferred_element_type=jnp.float32).astype(jnp.bfloat16)
        for i in range(n_tp - 1):
            partial[rest + i, t] = y[i * cap : (i + 1) * cap]

        @pl.when((z == 0) & (t < near))
        def _():
            right_copy(n_tp - 2, t).start()

        @pl.when((z == n_tp - 1) & (t < near))
        def _():
            left_copy(1, t).start()

    each_tile(project_rest)

    for j in range(2, n_tp - 1):

        def send_more(t):
            @pl.when(z == 0)
            def _():
                right_copy(n_tp - 1 - j, t).start()

            @pl.when(z == n_tp - 1)
            def _():
                left_copy(j, t).start()

        each_tile(send_more, 0, near)

    def pump(j, t):
        d_right = n_tp - 1 - j
        d_left = j

        @pl.when((z > 0) & (z < d_right) & ((t < near) | (z > 1)))
        def _():
            cp = right_copy(d_right, t)
            cp.wait_recv()
            partial[d_right, t] = (
                partial[d_right, t].astype(jnp.float32)
                + landed[d_right + 1, t].astype(jnp.float32)
            ).astype(jnp.bfloat16)
            cp.start()

        @pl.when((z < n_tp - 1) & (z > d_left) & ((t < near) | (z < n_tp - 2)))
        def _():
            cp = left_copy(d_left, t)
            cp.wait_recv()
            partial[d_left, t] = (
                partial[d_left, t].astype(jnp.float32)
                + landed[d_left, t].astype(jnp.float32)
            ).astype(jnp.bfloat16)
            cp.start()

    each_tile(functools.partial(pump, 0), 0, near)

    @pl.when(helper)
    def _():
        for f in range(FAR_TILES):
            for r in range(2, n_ctx, 2):
                spread_copy(r, f).wait_recv()
                mate_weights(r, f).start()

    each_tile(functools.partial(pump, 1), 0, near)

    @pl.when(helper)
    def _():
        base = jnp.where(z == 1, 1, 0)
        for f in range(FAR_TILES):
            for r in range(1, n_ctx, 2):
                spread_copy(r, f).wait_recv()
        for i in range(n_tp - 1):
            far_copy(base + i).wait_recv()

        def far_tile(t):
            a = attfar[pl.ds(base, n_tp - 1)].reshape((n_tp - 1) * cap, attended.shape[2])
            y = jnp.dot(a, wfar[t - near], preferred_element_type=jnp.float32)
            for i in range(n_tp - 1):
                d = base + i
                partial[d, t] = (
                    partial[d, t].astype(jnp.float32) + y[i * cap : (i + 1) * cap]
                ).astype(jnp.bfloat16)

        each_tile(far_tile, near, tiles)

        for j in range(n_tp - 2):

            def far_send_on(t):
                @pl.when(z == 1)
                def _():
                    right_copy(n_tp - 1 - j, t).start()

                @pl.when(z == n_tp - 2)
                def _():
                    left_copy(j, t).start()

            each_tile(far_send_on, near, tiles)

    for j in range(2, n_tp - 1):
        each_tile(functools.partial(pump, j), 0, near)
    for j in range(n_tp - 1):
        each_tile(functools.partial(pump, j), near, tiles)

    def finish(t, squares):
        cols = pl.ds(pl.multiple_of(t * TILE, TILE), TILE)
        hid_ref[:, cols] = res_ref[:, cols].astype(jnp.float32) + partial[z, t].astype(jnp.float32)

        @pl.when((z > 0) & ((t < near) | (z > 1)))
        def _():
            right_copy(z, t).wait_recv()
            hid_ref[:, cols] = hid_ref[:, cols] + landed[z + 1, t].astype(jnp.float32)

        @pl.when((z < n_tp - 1) & ((t < near) | (z < n_tp - 2)))
        def _():
            left_copy(z, t).wait_recv()
            hid_ref[:, cols] = hid_ref[:, cols] + landed[z, t].astype(jnp.float32)

        h = hid_ref[:, cols]
        return squares + jnp.sum(h * h, axis=-1, keepdims=True)

    squares = lax.fori_loop(0, tiles, finish, jnp.zeros((cap, 1), jnp.float32))
    inv_ref[...] = jnp.broadcast_to(lax.rsqrt(squares / (tiles * TILE) + 1e-05), inv_ref.shape)

    for r in strides:

        @pl.when(c + r < n_ctx)
        def _():
            for cp in own_copies(r):
                cp.wait_send()

        @pl.when(c >= r)
        def _():
            if r < window:

                @pl.when(even)
                def _():
                    for cp in forward_copies(r, window - r - 1):
                        cp.wait_send()

            @pl.when(jnp.logical_not(even))
            def _():
                for cp in forward_copies(r, window - r + 1):
                    cp.wait_send()

    @pl.when(even)
    def _():
        for cp in mate_copies():
            cp.wait_send()

    for d in range(n_tp):

        def sent(t):
            @pl.when((z < d) & ((t < near) | (z > 0)))
            def _():
                right_copy(d, t).wait_send()

            @pl.when((z > d) & ((t < near) | (z < n_tp - 1)))
            def _():
                left_copy(d, t).wait_send()

        each_tile(sent)

    @pl.when(at_end)
    def _():
        for f in range(FAR_TILES):
            ship_copy(f).wait_send()
        for i in range(n_tp - 1):
            far_copy(jnp.where(z == 0, n_tp - 1 - i, i)).wait_send()

    @pl.when(helper)
    def _():
        for f in range(FAR_TILES):
            mate_weights(0, f).wait_send()
            for r in range(2, n_ctx, 2):
                spread_copy(r, f).wait_send()
                mate_weights(r, f).wait_send()


def scale_rows(hidden_ref, inverse_ref, gain_ref, hid_ref, norm_ref):
    h = hidden_ref[...]
    hid_ref[...] = h.astype(hid_ref.dtype)
    norm_ref[...] = (h * inverse_ref[:, :1] * gain_ref[...]).astype(norm_ref.dtype)


def on_device(n_ctx, n_tp, queries, key_rows, value_rows, segments, owner_ids, out_proj, residual, norm_gain):
    rows, width = queries.shape
    cap, model = residual.shape
    tiles = model // TILE
    keys = (n_ctx // 2 + 1) * rows
    vmem = pl.BlockSpec(memory_space=pltpu.VMEM)
    hidden, inverse = pl.pallas_call(
        functools.partial(kernel, n_ctx, n_tp),
        out_shape=(
            jax.ShapeDtypeStruct((cap, model), jnp.float32),
            jax.ShapeDtypeStruct((cap, HEAD_DIM), jnp.float32),
        ),
        in_specs=[vmem] * 5 + [pl.BlockSpec(memory_space=pl.ANY), vmem],
        out_specs=(vmem, vmem),
        scratch_shapes=[
            pltpu.VMEM((keys, key_rows.shape[1]), jnp.bfloat16),
            pltpu.VMEM((keys, key_rows.shape[1]), jnp.bfloat16),
            pltpu.VMEM((tiles, width, TILE), jnp.bfloat16),
            pltpu.VMEM((n_tp, cap, width), jnp.bfloat16),
            pltpu.VMEM((n_tp, tiles, cap, TILE), jnp.bfloat16),
            pltpu.VMEM((n_tp + 1, tiles, cap, TILE), jnp.bfloat16),
            pltpu.VMEM((FAR_TILES, width, TILE), jnp.bfloat16),
            pltpu.VMEM((n_tp, cap, width), jnp.bfloat16),
            pltpu.SemaphoreType.DMA((n_ctx // 2 + 1, 2)),
            pltpu.SemaphoreType.DMA((n_ctx // 2 + 1, 2)),
            pltpu.SemaphoreType.DMA((n_ctx // 2 + 1, 2)),
            pltpu.SemaphoreType.DMA((tiles,)),
            pltpu.SemaphoreType.DMA((n_tp, tiles)),
            pltpu.SemaphoreType.DMA((n_tp + 1, tiles)),
            pltpu.SemaphoreType.DMA((FAR_TILES,)),
            pltpu.SemaphoreType.DMA((n_ctx, FAR_TILES)),
            pltpu.SemaphoreType.DMA((n_ctx, FAR_TILES)),
            pltpu.SemaphoreType.DMA((n_tp,)),
            pltpu.SemaphoreType.DMA((n_tp,)),
        ],
        compiler_params=pltpu.CompilerParams(
            collective_id=0, has_side_effects=True, vmem_limit_bytes=60 * 1024 * 1024
        ),
    )(
        queries,
        key_rows,
        value_rows,
        segments.reshape(n_ctx, 1, rows),
        owner_ids.reshape(1, rows),
        out_proj,
        residual,
    )
    out = jax.ShapeDtypeStruct((cap, model), jnp.bfloat16)
    part = pl.BlockSpec((16, model), lambda i: (i, 0))
    return pl.pallas_call(
        scale_rows,
        grid=(cap // 16,),
        out_shape=(out, out),
        in_specs=[
            part,
            pl.BlockSpec((16, HEAD_DIM), lambda i: (i, 0)),
            pl.BlockSpec((1, model), lambda i: (0, 0)),
        ],
        out_specs=(part, part),
    )(hidden, inverse, norm_gain.reshape(1, model))


def solution(mesh):
    placed = (
        P("ctx", "tp"),
        P("ctx", "tp"),
        P("ctx", "tp"),
        P(),
        P("ctx", None),
        P("tp", None),
        P(("ctx", "tp"), None),
        P(),
    )
    return jax.shard_map(
        functools.partial(on_device, mesh.shape["ctx"], mesh.shape["tp"]),
        mesh=mesh,
        in_specs=placed,
        out_specs=(P(("ctx", "tp"), None), P(("ctx", "tp"), None)),
        check_vma=False,
    )
```
